512 devices in a mesh: head: 32 (over y, x, core), ctx: 16 (over z).
Axes of the slice: x: 4, y: 4, z: 16, core: 2. Of those that a mesh axis runs over, the one named last changes fastest.
Arguments:
- queries: bfloat16 [65536, 4096], P(('ctx', 'head')), may hold values from -30 to 30
- keys: bfloat16 [65536, 4096], P(('ctx', 'head')), may hold values from -6 to 6
- values: bfloat16 [65536, 4096], P(('ctx', 'head')), may hold values from -6 to 6
- pattern: int32 [512, 5], replicated, may hold values from 0 to 511, as said below
Outputs:
- attended: bfloat16 [65536, 4096], P(('ctx', 'head'))
The draws below stay inside these ranges and needn't reach their ends.
Inputs may be any that keep to these rules, and one draw needn't show every extreme that they name: `pattern`: row a lists 5 different query blocks, none of them a. The entries of the 32 rows c * 32 to (c + 1) * 32 - 1 name the blocks d * 32 to (d + 1) * 32 - 1 exactly 10 times, for every c and d.
All inputs are finite; a program needn't handle non-finite values.
Results may differ from the reference program's by a relative error of at most 0.0075.
Values may be sent and summed in bfloat16 or wider, within the bound.
No kernel may reach another device: no remote copies, remote signals or barrier semaphores. Data moves between devices by JAX's collectives and lax.ppermute only.
A program may use at most 128 MiB of HBM per device.

```python
import jax
import jax.numpy as jnp
from jax import lax

D = 4096
HEADS = 32
HD = 128
BLOCK = 128
QPER = 5
KB_DEV = 32
BLOCKS = 512
WORDS = 65536
CAP = 10


def paired_rows(key):
    key_query = jax.random.fold_in(key, 11)
    key_keys = jax.random.fold_in(key, 12)
    query_rows = jnp.clip(jax.random.normal(key_query, (WORDS, D), jnp.float32), -6.0, 6.0)
    key_rows = jnp.clip(jax.random.normal(key_keys, (WORDS, D), jnp.float32), -6.0, 6.0)
    return (query_rows, key_rows)


def draw_queries(key, part):
    return paired_rows(key)[0].astype(jnp.bfloat16)


def draw_keys(key, part):
    return paired_rows(key)[1].astype(jnp.bfloat16)


def draw_pattern(key, part):
    shards = BLOCKS // KB_DEV
    per_owner = KB_DEV * QPER
    index = jnp.arange(BLOCKS, dtype=jnp.int32)
    owner = index // KB_DEV
    inside = index % KB_DEV
    orders = jax.vmap(lambda shard: jax.random.permutation(jax.random.fold_in(key, 100 + shard), per_owner))(jnp.arange(shards, dtype=jnp.int32))
    entry = inside[:, None] * QPER + jnp.arange(QPER, dtype=jnp.int32)[None, :]
    target = orders[owner[:, None], entry].astype(jnp.int32) // CAP
    offset = jax.random.randint(jax.random.fold_in(key, 7), (BLOCKS, 1), 0, KB_DEV - 1)
    within = (inside[:, None] + 1 + (offset + jnp.arange(QPER, dtype=jnp.int32)[None, :]) % (KB_DEV - 1)) % KB_DEV
    return (target * KB_DEV + within).astype(jnp.int32)


def levels(key, extent, cuts, least, largest):
    def one(dim, blocks):
        steps = jax.random.uniform(jax.random.fold_in(jax.random.fold_in(key, 6), dim), (blocks,), jnp.float32, least / len(cuts), largest / len(cuts))
        return jnp.repeat(jnp.exp(steps), extent[dim] // blocks).reshape((-1,) + (1,) * (len(extent) - dim - 1))

    loudness = one(*cuts[0])
    for cut in cuts[1:]:
        loudness = loudness * one(*cut)
    return loudness


def bell_draw(key, dims, spread, most, split=(), kind=jnp.bfloat16):
    factor_of = levels(key, dims, split, -0.22, 0.18) if split else 1.0
    drawn = jax.random.normal(key, dims, jnp.float32) * spread * factor_of
    return jnp.minimum(jnp.maximum(drawn, -most), most).astype(kind)


def setup_inputs(seed: int = 0) -> dict:
    key_of = jax.random.split(jax.random.key(seed), 5)
    return {
        "queries": draw_queries(jax.random.fold_in(key_of[4], 71), 0),
        "keys": draw_keys(jax.random.fold_in(key_of[4], 71), 0),
        "values": bell_draw(key_of[2], (WORDS, D), 1.0, 6.0, ((0, 512),)),
        "pattern": draw_pattern(jax.random.fold_in(key_of[4], 71), 0),
    }


def reference(queries, keys, values, pattern):
    count = WORDS // BLOCK
    scale = HD ** -0.5
    query_all = queries.reshape(count, BLOCK, HEADS, HD)
    key_all = keys.reshape(count, BLOCK, HEADS, HD)
    value_all = values.reshape(count, BLOCK, HEADS, HD)
    listed = jnp.concatenate([jnp.arange(count, dtype=jnp.int32)[:, None], pattern.astype(jnp.int32)], axis=1)

    def step(carry, index):
        best, denom, numer = carry
        chosen = listed[index]
        query_sel = query_all[chosen].astype(jnp.float32)
        key_here = key_all[index].astype(jnp.float32)
        value_here = value_all[index].astype(jnp.float32)
        scores = jnp.einsum("jqhd,khd->jhqk", query_sel, key_here) * scale
        peak = jnp.max(scores, axis=-1)
        expo = jnp.exp(scores - peak[..., None])
        total = jnp.sum(expo, axis=-1)
        weights = expo.astype(jnp.bfloat16).astype(jnp.float32)
        mixed = jnp.einsum("jhqk,khd->jqhd", weights, value_here)
        partial_out = (mixed / jnp.transpose(total, (0, 2, 1))[..., None]).astype(jnp.bfloat16).astype(jnp.float32)
        level = jnp.transpose(peak + jnp.log(total), (0, 2, 1))
        old_best = best[chosen]
        new_best = jnp.maximum(old_best, level)
        keep_old = jnp.exp(old_best - new_best)
        take_new = jnp.exp(level - new_best)
        best = best.at[chosen].set(new_best)
        denom = denom.at[chosen].set(denom[chosen] * keep_old + take_new)
        numer = numer.at[chosen].set(numer[chosen] * keep_old[..., None] + take_new[..., None] * partial_out)
        return (best, denom, numer), None

    start = (jnp.full((count, BLOCK, HEADS), -1e30, jnp.float32),
             jnp.zeros((count, BLOCK, HEADS), jnp.float32),
             jnp.zeros((count, BLOCK, HEADS, HD), jnp.float32))
    (best, denom, numer), unused = lax.scan(step, start, jnp.arange(count, dtype=jnp.int32))
    return (numer / denom[..., None]).astype(jnp.bfloat16).reshape(WORDS, D)
```

```python
import functools

import jax
import jax.numpy as jnp
import numpy as np
from jax import lax
from jax.experimental import pallas as pl
from jax.experimental.pallas import tpu as pltpu
from jax.sharding import Mesh, PartitionSpec as P

HD = 128
BLOCK = 128
QPER = 5
AXES = ("yh", "yl", "xh", "xl", "core")
SPLIT = "yh"
GROUP = tuple(a for a in AXES if a != SPLIT)
OWN = 32
GANG = 8
ROOM = 168
CHUNKS = 384
DEPTH = 4
SCALE = float(np.log2(np.e)) * HD**-0.5


def list_kernel(code, mine, slots, bases, metas, count, filled):
    entries = code.shape[0]

    def start(q, carry):
        filled[q] = 1
        slots[q * ROOM] = mine[q]
        return carry

    lax.fori_loop(0, OWN, start, 0)
    filled[OWN] = 0

    def place(a, carry):
        key = mine[OWN + a]
        for j in range(QPER):
            q = code[a * QPER + j]
            at = filled[q]
            slots[q * ROOM + at] = key
            filled[q] = at + 1
        return carry

    lax.fori_loop(0, entries // QPER, place, 0)

    def cut(q, total):
        have = filled[q]
        gangs = (have + GANG - 1) // GANG

        def pad(i, carry):
            slots[q * ROOM + i] = mine[q]
            return carry

        lax.fori_loop(have, gangs * GANG, pad, 0)

        def gang(g, carry):
            left = jnp.minimum(have - g * GANG, GANG)
            bases[total + g] = q * ROOM + g * GANG
            metas[total + g] = ((q * 16 + left) * 2 + (g == 0).astype(jnp.int32)) * 2 + (
                g == gangs - 1
            ).astype(jnp.int32)
            return carry

        lax.fori_loop(0, gangs, gang, 0)
        return total + gangs

    count[0] = lax.fori_loop(0, OWN, cut, 0)


def pair_lists(code, mine):
    smem = pl.BlockSpec(memory_space=pltpu.SMEM)
    return pl.pallas_call(
        list_kernel,
        in_specs=[smem, smem],
        out_specs=[smem] * 4,
        out_shape=[
            jax.ShapeDtypeStruct((OWN * ROOM + code.shape[0],), jnp.int32),
            jax.ShapeDtypeStruct((CHUNKS,), jnp.int32),
            jax.ShapeDtypeStruct((CHUNKS,), jnp.int32),
            jax.ShapeDtypeStruct((8,), jnp.int32),
        ],
        scratch_shapes=[pltpu.SMEM((OWN + 1,), jnp.int32)],
        cost_estimate=pl.CostEstimate(flops=0, bytes_accessed=60_000_000, transcendentals=0),
    )(code, mine)


def attend_kernel(slots, bases, metas, count, q, k, vt, o, kbuf, vbuf, acc, peak, total, sem):
    gangs = count[0]
    acc[...] = jnp.zeros_like(acc)
    total[...] = jnp.zeros_like(total)
    peak[...] = jnp.zeros_like(peak)

    def copies(t):
        at = lax.rem(t, DEPTH)
        base = bases[t]
        made = []
        for j in range(GANG):
            key = slots[base + j]
            part = pl.ds(j * BLOCK, BLOCK)
            made.append(pltpu.make_async_copy(k.at[key], kbuf.at[at, part], sem.at[at, 0, j]))
            made.append(pltpu.make_async_copy(vt.at[key], vbuf.at[at, :, part], sem.at[at, 1, j]))
        return made

    def fetch(t):
        @pl.when(t < gangs)
        def _():
            for copy in copies(t):
                copy.start()

    for t in range(DEPTH - 1):
        fetch(t)

    def step(t, carry):
        fetch(t + DEPTH - 1)
        for copy in copies(t):
            copy.wait()
        at = lax.rem(t, DEPTH)
        meta = metas[t]
        last = lax.rem(meta, 2)
        first = lax.rem(meta // 2, 2)
        left = lax.rem(meta // 4, 16)
        mine = meta // 64
        scores = lax.dot_general(
            kbuf[at], q[mine], (((1,), (1,)), ((), ())), preferred_element_type=jnp.float32
        )
        row = lax.broadcasted_iota(jnp.int32, scores.shape, 0)
        scores = jnp.where(row < left * BLOCK, scores * SCALE, -1e30)
        old = jnp.where(first == 1, jnp.full((1, HD), -1e30, jnp.float32), peak[0:1])
        new = jnp.maximum(old, jnp.max(scores, axis=0, keepdims=True))
        expo = jnp.exp2(scores - new)
        keep = jnp.exp2(old - new)
        total_new = total[0:1] * keep + jnp.sum(expo, axis=0, keepdims=True)
        mixed = jnp.dot(vbuf[at], expo.astype(jnp.bfloat16), preferred_element_type=jnp.float32)
        acc_new = acc[...] * keep + mixed
        peak[0:1] = new
        total[0:1] = total_new
        acc[...] = acc_new

        @pl.when(last == 1)
        def _():
            o[mine] = (acc_new / total_new).T.astype(jnp.bfloat16)

        return carry

    lax.fori_loop(0, gangs, step, 0)


def attend(lists, q, k, vt):
    vmem = pl.BlockSpec((OWN, BLOCK, HD), lambda i, *_: (0, 0, 0))
    anywhere = pl.BlockSpec(memory_space=pl.ANY)
    return pl.pallas_call(
        attend_kernel,
        grid_spec=pltpu.PrefetchScalarGridSpec(
            num_scalar_prefetch=4,
            grid=(1,),
            in_specs=[vmem, anywhere, anywhere],
            out_specs=vmem,
            scratch_shapes=[
                pltpu.VMEM((DEPTH, GANG * BLOCK, HD), jnp.bfloat16),
                pltpu.VMEM((DEPTH, HD, GANG * BLOCK), jnp.bfloat16),
                pltpu.VMEM((HD, BLOCK), jnp.float32),
                pltpu.VMEM((8, BLOCK), jnp.float32),
                pltpu.VMEM((8, BLOCK), jnp.float32),
                pltpu.SemaphoreType.DMA((DEPTH, 2, GANG)),
            ],
        ),
        out_shape=jax.ShapeDtypeStruct((OWN, BLOCK, HD), jnp.bfloat16),
        compiler_params=pltpu.CompilerParams(vmem_limit_bytes=50 << 20),
        cost_estimate=pl.CostEstimate(
            flops=200 * 4 * BLOCK**3, bytes_accessed=20 << 20, transcendentals=200 * BLOCK**2
        ),
    )(*lists, q, k, vt)


def place_of(block):
    ctx, rest = block // 32, block % 32
    rank, split = jnp.zeros_like(block), jnp.zeros_like(block)
    for i, axis in enumerate(AXES):
        bit = (rest >> (len(AXES) - 1 - i)) & 1
        if axis == SPLIT:
            split = bit
        else:
            rank = rank * 2 + bit
    return rank, ctx * 2 + split


def body(queries, keys, values, pattern):
    exchange = ("ctx", SPLIT)

    def to_heads(x):
        return lax.all_to_all(x, exchange, split_axis=1, concat_axis=0, tiled=True)

    me = jnp.int32(0)
    for axis in GROUP:
        me = me * 2 + lax.axis_index(axis)
    rank, slot = place_of(pattern.reshape(-1))
    code = jnp.where(rank == me, slot, OWN)
    rank, slot = place_of(jnp.arange(pattern.shape[0], dtype=jnp.int32))
    mine = jnp.concatenate([me * OWN + jnp.arange(OWN, dtype=jnp.int32), rank * OWN + slot])

    key_rows = to_heads(keys)
    key_rows, values = lax.optimization_barrier((key_rows, values))
    key_all = lax.all_gather(key_rows.reshape(OWN, BLOCK, HD), GROUP, axis=0, tiled=True)
    value_rows = to_heads(values)
    value_rows, queries = lax.optimization_barrier((value_rows, queries))
    turned = jnp.swapaxes(value_rows.reshape(OWN, BLOCK, HD), 1, 2)
    value_all = lax.all_gather(turned, GROUP, axis=0, tiled=True)
    query_rows = to_heads(queries).reshape(OWN, BLOCK, HD)
    out = attend(pair_lists(code, mine), query_rows, key_all, value_all)
    return lax.all_to_all(
        out.reshape(OWN * BLOCK, HD), exchange, split_axis=0, concat_axis=1, tiled=True
    )


def solution(mesh):
    fine = Mesh(mesh.devices.reshape(2, 2, 2, 2, 2, 16), AXES + ("ctx",))
    rows = P(("ctx",) + AXES, None)
    return jax.shard_map(
        body, mesh=fine, in_specs=(rows, rows, rows, P()), out_specs=rows, check_vma=False
    )
```

```python
import jax
import jax.numpy as jnp
import numpy as np
from jax import lax
from jax.experimental import pallas as pl
from jax.experimental.pallas import tpu as pltpu
from jax.sharding import Mesh, PartitionSpec as P

HD = 128
BLOCK = 128
QPER = 5
AXES = ("yh", "yl", "xh", "xl", "core")
SPLIT = "yh"
PAIR = "yl"
GROUP = ("xh", "xl", "core")
OWN = 32
GANG = 4
ROOM = 168
WIDTH = 8
GANGS = 680
DEPTH = 6
SCALE = float(np.log2(np.e)) * HD**-0.5
LOW = -1e30


def list_kernel(code, spot, theirs, ours, slots, filled):
    def start(q, carry):
        filled[q] = 0
        filled[OWN + q] = 1
        slots[(OWN + q) * ROOM] = spot[q]
        return carry

    lax.fori_loop(0, OWN, start, 0)
    filled[2 * OWN] = 0

    def place(a, carry):
        key = spot[OWN + a]
        for j in range(QPER):
            q = code[a * QPER + j]
            at = filled[q]
            slots[q * ROOM + at] = key
            filled[q] = at + 1
        return carry

    lax.fori_loop(0, code.shape[0] // QPER, place, 0)

    for side, plan in ((0, theirs), (1, ours)):

        def cut(q, total):
            row = side * OWN + q
            have = filled[row]
            gangs = jnp.maximum((have + GANG - 1) // GANG, 1)
            spare = spot[q]

            def gang(g, carry):
                left = have - g * GANG
                for j in range(GANG):
                    key = slots[row * ROOM + g * GANG + j]
                    plan[(total + g) * WIDTH + j] = jnp.where(j < left, key, spare)
                plan[(total + g) * WIDTH + GANG] = q
                plan[(total + g) * WIDTH + GANG + 1] = left
                plan[(total + g) * WIDTH + GANG + 2] = (g == 0).astype(jnp.int32)
                return carry

            lax.fori_loop(0, gangs, gang, 0)
            return total + gangs

        plan[GANGS * WIDTH] = lax.fori_loop(0, OWN, cut, 0)


def pair_lists(code, spot):
    smem = pl.BlockSpec(memory_space=pltpu.SMEM)
    return pl.pallas_call(
        list_kernel,
        in_specs=[smem, smem],
        out_specs=[smem] * 2,
        out_shape=[jax.ShapeDtypeStruct((GANGS * WIDTH + WIDTH,), jnp.int32)] * 2,
        scratch_shapes=[
            pltpu.SMEM((2 * OWN * ROOM + code.shape[0] + WIDTH,), jnp.int32),
            pltpu.SMEM((2 * OWN + 1,), jnp.int32),
        ],
        cost_estimate=pl.CostEstimate(flops=0, bytes_accessed=60_000_000, transcendentals=0),
    )(code, spot)


def attend_kernel(plan, q, kv, o, level, kbuf, vbuf, expo, acc, peak, keep, sums, total, sem):
    gangs = plan[GANGS * WIDTH]
    acc[...] = jnp.zeros_like(acc)
    total[...] = jnp.zeros_like(total)
    peak[...] = jnp.full_like(peak, LOW)

    def copies(t):
        at = lax.rem(t, DEPTH)
        base = jnp.minimum(t, gangs - 1) * WIDTH
        made = []
        for j in range(GANG):
            key = plan[base + j]
            part = pl.ds(j * BLOCK, BLOCK)
            made.append(
                pltpu.make_async_copy(
                    kv.at[key, pl.ds(0, BLOCK)], kbuf.at[at, part], sem.at[at, 0, j]
                )
            )
            made.append(
                pltpu.make_async_copy(
                    kv.at[key, pl.ds(BLOCK, HD)], vbuf.at[at, :, part], sem.at[at, 1, j]
                )
            )
        return made

    def fetch(t):
        for copy in copies(t):
            copy.start()

    def wait(t):
        for copy in copies(t):
            copy.wait()

    def weigh(t):
        at, side = lax.rem(t, DEPTH), lax.rem(t, 2)
        base = jnp.minimum(t, gangs - 1) * WIDTH
        row, left, first = plan[base + GANG], plan[base + GANG + 1], plan[base + GANG + 2]
        scores = lax.dot_general(
            kbuf[at], q[row], (((1,), (1,)), ((), ())), preferred_element_type=jnp.float32
        )
        parts = []
        for j in range(GANG):
            bias = jnp.where(j < left, 0.0, LOW)
            parts.append(scores[j * BLOCK : (j + 1) * BLOCK] * SCALE + bias)
        most = parts[0]
        for part in parts[1:]:
            most = jnp.maximum(most, part)
        old = jnp.where(first == 1, LOW, peak[1 - side, 0:1])
        new = jnp.maximum(old, jnp.max(most, axis=0, keepdims=True))
        summed = None
        for j, part in enumerate(parts):
            raised = jnp.exp2(part - new)
            expo[side, pl.ds(j * BLOCK, BLOCK)] = raised.astype(jnp.bfloat16)
            summed = raised if summed is None else summed + raised
        peak[side, 0:1] = new
        keep[side, 0:1] = jnp.exp2(old - new)
        sums[side, 0:1] = jnp.sum(summed, axis=0, keepdims=True)

    def mix(t):
        at, side = lax.rem(t, DEPTH), lax.rem(t, 2)
        row = plan[t * WIDTH + GANG]
        mixed = jnp.dot(vbuf[at], expo[side], preferred_element_type=jnp.float32)
        kept = keep[side, 0:1]
        whole = total[0:1] * kept + sums[side, 0:1]
        value = acc[...] * kept + mixed
        total[0:1] = whole
        acc[...] = value
        o[row] = (value * (1.0 / whole)).astype(o.dtype)
        level[row] = peak[side, 0:1] + jnp.log2(whole)

    for t in range(DEPTH - 2):
        fetch(t)
    wait(0)
    weigh(0)

    def step(t, carry):
        fetch(t + DEPTH - 2)
        wait(t + 1)
        mix(t)
        weigh(t + 1)
        return carry

    lax.fori_loop(0, gangs, step, 0)
    for extra in range(1, DEPTH - 2):
        wait(gangs + extra)


def attend(plan, q, kv, kind):
    anywhere = pl.BlockSpec(memory_space=pl.ANY)
    row = pltpu.VMEM((2, 8, BLOCK), jnp.float32)
    return pl.pallas_call(
        attend_kernel,
        grid_spec=pltpu.PrefetchScalarGridSpec(
            num_scalar_prefetch=1,
            grid=(1,),
            in_specs=[pl.BlockSpec((OWN, BLOCK, HD), lambda i, *_: (0, 0, 0)), anywhere],
            out_specs=[
                pl.BlockSpec((OWN, HD, BLOCK), lambda i, *_: (0, 0, 0)),
                pl.BlockSpec((OWN, 1, BLOCK), lambda i, *_: (0, 0, 0)),
            ],
            scratch_shapes=[
                pltpu.VMEM((DEPTH, GANG * BLOCK, HD), jnp.bfloat16),
                pltpu.VMEM((DEPTH, HD, GANG * BLOCK), jnp.bfloat16),
                pltpu.VMEM((2, GANG * BLOCK, BLOCK), jnp.bfloat16),
                pltpu.VMEM((HD, BLOCK), jnp.float32),
                row,
                row,
                row,
                pltpu.VMEM((8, BLOCK), jnp.float32),
                pltpu.SemaphoreType.DMA((DEPTH, 2, GANG)),
            ],
        ),
        out_shape=[
            jax.ShapeDtypeStruct((OWN, HD, BLOCK), kind),
            jax.ShapeDtypeStruct((OWN, 1, BLOCK), jnp.float32),
        ],
        compiler_params=pltpu.CompilerParams(vmem_limit_bytes=50 << 20),
        cost_estimate=pl.CostEstimate(
            flops=100 * 4 * BLOCK**3, bytes_accessed=40 << 20, transcendentals=100 * BLOCK**2
        ),
    )(plan, q, kv)


def combine_kernel(mine, my_level, other, other_level, o):
    for q in range(OWN):
        a, b = my_level[q], other_level[q]
        top = jnp.maximum(a, b)
        share_a, share_b = jnp.exp2(a - top), jnp.exp2(b - top)
        scale = 1.0 / (share_a + share_b)
        value = mine[q] * (share_a * scale) + other[q].astype(jnp.float32) * (share_b * scale)
        o[q] = value.T.astype(o.dtype)


def combine(*parts):
    return pl.pallas_call(
        combine_kernel,
        out_shape=jax.ShapeDtypeStruct((OWN, BLOCK, HD), jnp.bfloat16),
        compiler_params=pltpu.CompilerParams(vmem_limit_bytes=32 << 20),
        cost_estimate=pl.CostEstimate(flops=0, bytes_accessed=8 << 20, transcendentals=0),
    )(*parts)


def pack_kernel(keys, values, o):
    for n in range(o.shape[0]):
        part = pl.ds(n * HD, HD)
        o[n, pl.ds(0, BLOCK)] = keys[:, part]
        o[n, pl.ds(BLOCK, HD)] = values[:, part].T


def pack(keys, values):
    heads, step = keys.shape[1] // HD, 8
    rows = pl.BlockSpec((BLOCK, step * HD), lambda i: (0, i))
    return pl.pallas_call(
        pack_kernel,
        grid=(heads // step,),
        in_specs=[rows, rows],
        out_specs=pl.BlockSpec((step, BLOCK + HD, HD), lambda i: (i, 0, 0)),
        out_shape=jax.ShapeDtypeStruct((heads, BLOCK + HD, HD), keys.dtype),
        cost_estimate=pl.CostEstimate(flops=0, bytes_accessed=4 << 20, transcendentals=0),
    )(keys, values)


def place_of(block):
    ctx, rest = block // 32, block % 32
    pair, rank, split = (jnp.zeros_like(block) for _ in range(3))
    for i, axis in enumerate(AXES):
        bit = (rest >> (len(AXES) - 1 - i)) & 1
        if axis == SPLIT:
            split = bit
        elif axis == PAIR:
            pair = bit
        else:
            rank = rank * 2 + bit
    return pair, rank, ctx * 2 + split


def pair_codes(pattern, my_pair, my_rank):
    key_pair, key_rank, key_slot = place_of(jnp.arange(pattern.shape[0], dtype=jnp.int32))
    pair, rank, slot = place_of(pattern)
    here = (key_pair[:, None] == my_pair) & (rank == my_rank)
    code = jnp.where(here, slot + OWN * (pair == my_pair), 2 * OWN)
    spot = jnp.concatenate(
        [my_rank * OWN + jnp.arange(OWN, dtype=jnp.int32), key_rank * OWN + key_slot]
    )
    return code.reshape(-1).astype(jnp.int32), spot


def body(queries, keys, values, pattern):
    exchange = ("ctx", SPLIT)
    heads = keys.shape[1] // HD

    def regroup(x):
        return lax.all_to_all(x, exchange, split_axis=0, concat_axis=0, tiled=True)

    def swap(x):
        return lax.ppermute(x, PAIR, [(0, 1), (1, 0)])

    my_rank = jnp.int32(0)
    for axis in GROUP:
        my_rank = my_rank * 2 + lax.axis_index(axis)
    plans = pair_lists(*pair_codes(pattern, lax.axis_index(PAIR), my_rank))

    split = (BLOCK, heads, HD)
    both = regroup(pack(keys, values))
    both, queries = lax.optimization_barrier((both, queries))
    gathered = lax.all_gather(both, GROUP, axis=0, tiled=True)
    mine = regroup(jnp.transpose(queries.reshape(split), (1, 0, 2)))
    other = swap(mine)
    for_other, other_level = attend(plans[0], other, gathered, jnp.bfloat16)
    from_other, from_level = swap(for_other), swap(other_level)
    own, own_level = attend(plans[1], mine, gathered, jnp.float32)
    out = regroup(combine(own, own_level, from_other, from_level))
    return jnp.transpose(out, (1, 0, 2)).reshape(queries.shape)


def solution(mesh):
    fine = Mesh(mesh.devices.reshape(2, 2, 2, 2, 2, 16), AXES + ("ctx",))
    rows = P(("ctx",) + AXES, None)
    return jax.shard_map(
        body, mesh=fine, in_specs=(rows, rows, rows, P()), out_specs=rows, check_vma=False
    )
```
